512 devices in a mesh: ctx: 32 (over y, z_lo), tp: 16 (over x, z_hi, core).
Axes of the slice: x: 4, y: 4, z: 16 (z_hi: 2, z_lo: 8; z = z_hi * 8 + z_lo), core: 2. Of those that a mesh axis runs over, the one named last changes fastest.
Arguments:
- tokens: bfloat16 [4096, 8192], P('ctx', 'tp'), may hold values from -6 to 6
- cotangent: bfloat16 [4096, 8192], P('ctx', 'tp'), may hold values from -6 to 6
- filters: bfloat16 [4096, 8192], P('ctx', 'tp'), may hold values from -0.09375 to 0.09375
Outputs:
- outputs: bfloat16 [4096, 8192], P('ctx', 'tp')
- input_grad: bfloat16 [4096, 8192], P('ctx', 'tp')
The draws below stay inside these ranges and needn't reach their ends.
All inputs are finite; a program needn't handle non-finite values.
Results may differ from the reference program's by a relative error of at most 0.012.
Values may be sent and summed in bfloat16 or wider, within the bound.
No kernel may reach another device: no remote copies, remote signals or barrier semaphores. Data moves between devices by JAX's collectives and lax.ppermute only.
A program may use at most 64 MiB of HBM per device.

```python
import jax
import jax.numpy as jnp
from jax import lax

C = 8192
TOKENS = 4096


def block_scale(stream_key, shape, shards, least, top_value):
    factor_of, own = 1.0, jax.random.fold_in(stream_key, 6)
    for dim, blocks in shards:
        heights = jnp.exp(jax.random.uniform(jax.random.fold_in(own, dim), (blocks,), jnp.float32, least / len(shards), top_value / len(shards)))
        factor_of = factor_of * jnp.repeat(heights, shape[dim] // blocks).reshape([-1 if axis == dim else 1 for axis in range(len(shape))])
    return factor_of


def centred(own_key, extent, spread, most, shards=(), kind=jnp.bfloat16):
    loudness = block_scale(own_key, extent, shards, -0.22, 0.18) if shards else 1.0
    entries = jax.random.normal(own_key, extent, jnp.float32) * spread * loudness
    return jnp.minimum(jnp.maximum(entries, -most), most).astype(kind)


def setup_inputs(seed: int = 0) -> dict:
    key_list = jax.random.split(jax.random.key(seed), 4)
    tokens = centred(key_list[0], (TOKENS, C), 1.0, 6.0, ((0, 32), (1, 16)))
    cotangent = centred(key_list[1], (TOKENS, C), 1.0, 6.0, ((0, 32), (1, 16)))
    filters = centred(key_list[2], (TOKENS, C), TOKENS ** -0.5, 0.09375, ((0, 32), (1, 16)))
    return dict(tokens=tokens, cotangent=cotangent, filters=filters)


def causal(field, filt):
    length = field.shape[0]
    total = 2 * length
    spec_field = jnp.fft.fft(field, n=total, axis=0)
    spec_filt = jnp.fft.fft(filt, n=total, axis=0)
    return jnp.real(jnp.fft.ifft(spec_field * spec_filt, axis=0))[:length]


def reference(tokens, cotangent, filters):
    tok_full = tokens.astype(jnp.float32)
    grad_full = cotangent.astype(jnp.float32)
    filt_full = filters.astype(jnp.float32)
    mirror_full = jnp.roll(filt_full, C // 2, axis=1)
    block_width = min(C, 512)
    blocks = C // block_width

    def one_block(index):
        start = index * block_width
        tok_part = lax.dynamic_slice_in_dim(tok_full, start, block_width, 1)
        grad_part = lax.dynamic_slice_in_dim(grad_full, start, block_width, 1)
        filt_part = lax.dynamic_slice_in_dim(filt_full, start, block_width, 1)
        mirror_part = lax.dynamic_slice_in_dim(mirror_full, start, block_width, 1)
        forward = causal(tok_part, filt_part) + causal(tok_part[::-1], mirror_part)[::-1]
        backward = causal(grad_part[::-1], filt_part)[::-1] + causal(grad_part, mirror_part)
        return forward, backward

    forward, backward = lax.map(one_block, jnp.arange(blocks, dtype=jnp.int32))
    forward = forward.transpose(1, 0, 2).reshape(TOKENS, C)
    backward = backward.transpose(1, 0, 2).reshape(TOKENS, C)
    return forward.astype(jnp.bfloat16), backward.astype(jnp.bfloat16)
```

```python
import math

import jax
import jax.numpy as jnp
import numpy as np
from jax import lax
from jax.experimental import pallas as pl
from jax.experimental.pallas import tpu as pltpu
from jax.sharding import Mesh
from jax.sharding import PartitionSpec as P

LANES = 128
BLOCKS = 32
TOTAL = 2 * LANES * BLOCKS
CH = 8
PARAMS = pltpu.CompilerParams(vmem_limit_bytes=40 * 2**20)


def tables():
    q = np.arange(BLOCKS)[:, None]
    m = np.arange(LANES)[None, :]
    turn = 2.0 * math.pi * (2 * q + 0.5) * m / TOTAL
    lane = np.arange(LANES)
    phase = 2.0 * math.pi * (lane[:, None] * lane[None, :] % LANES) / LANES
    cos, sin = np.cos(phase), np.sin(phase)
    ahead = np.block([[cos, -sin], [sin, cos]]).astype(np.float32)
    halves = []
    for matrix in (ahead, ahead.T):
        high = matrix.astype(jnp.bfloat16)
        low = (matrix - high.astype(np.float32)).astype(jnp.bfloat16)
        halves += [high, low]
    return np.cos(turn).astype(np.float32), np.sin(turn).astype(np.float32), np.stack(halves)


def rotate(value, angle):
    re, im = value
    eighth = round(angle / (math.pi / 4), 9) % 8
    root = math.sqrt(0.5)
    if eighth == 0:
        return re, im
    if eighth == 2:
        return -im, re
    if eighth == 4:
        return -re, -im
    if eighth == 6:
        return im, -re
    if eighth in (1, 3, 5, 7):
        plus, minus = (re + im) * root, (re - im) * root
        return {1: (minus, plus), 3: (-plus, minus), 5: (-minus, -plus), 7: (plus, -minus)}[eighth]
    cos, sin = math.cos(angle), math.sin(angle)
    return re * cos - im * sin, re * sin + im * cos


def dft(values, sign):
    size = len(values)
    if size == 1:
        return values
    if size == 2:
        (ar, ai), (br, bi) = values
        return [(ar + br, ai + bi), (ar - br, ai - bi)]
    radix = 4
    if size % 4 or size == 8:
        radix = 2
    rest = size // radix
    parts = [dft(values[i::radix], sign) for i in range(radix)]
    out = [None] * size
    for k in range(rest):
        turned = [rotate(parts[i][k], sign * 2.0 * math.pi * i * k / size) for i in range(radix)]
        if radix == 2:
            (ar, ai), (br, bi) = turned
            out[k], out[k + rest] = (ar + br, ai + bi), (ar - br, ai - bi)
        else:
            (ar, ai), (br, bi), (cr, ci), (dr, di) = turned
            er, ei, fr, fi = ar + cr, ai + ci, ar - cr, ai - ci
            gr, gi, hr, hi = br + dr, bi + di, (br - dr) * sign, (bi - di) * sign
            out[k] = er + gr, ei + gi
            out[k + rest] = fr - hi, fi + hr
            out[k + 2 * rest] = er - gr, ei - gi
            out[k + 3 * rest] = fr + hi, fi - hr
    return out


def product(left, matrix_high, matrix_low):
    high = left.astype(jnp.bfloat16)
    low = (left - high.astype(jnp.float32)).astype(jnp.bfloat16)
    dot = lambda a, b: jnp.dot(a, b, preferred_element_type=jnp.float32)
    return dot(high, matrix_high) + (dot(low, matrix_high) + dot(high, matrix_low))


def gather_kernel(tok_ref, grad_ref, filt_ref, out_ref):
    for pair in range(out_ref.shape[0] // (6 * CH)):
        if pair % 8 == 0:
            cols = pl.ds(pair * 2 * CH, LANES)
            turned = [ref[:, cols].astype(jnp.float32).T for ref in (tok_ref, grad_ref, filt_ref)]
        at = (pair % 8) * 2 * CH
        rows = [part[at + CH * i : at + CH * (i + 1)] for i in range(2) for part in turned]
        out_ref[pl.ds(pair * 6 * CH, 6 * CH), :] = jnp.concatenate(rows).astype(jnp.bfloat16)


def scatter_kernel(in_ref, out_ref, grad_ref):
    for block in range(out_ref.shape[1] // LANES):
        rows = LANES // CH
        held = in_ref[pl.ds(block * 2 * LANES, 2 * LANES), :].astype(jnp.float32)
        held = held.reshape(rows, 2, CH, LANES)
        for i, ref in enumerate((out_ref, grad_ref)):
            part = held[:, i].reshape(LANES, LANES).T
            ref[:, pl.ds(block * LANES, LANES)] = part.astype(jnp.bfloat16)


def operator_kernel(in_ref, cos_ref, sin_ref, mat_ref, out_ref, work, spec):
    for half in range(2):
        slabs = []
        for n in range(BLOCKS):
            held = in_ref[pl.ds(n * 6 * CH, 6 * CH), :].astype(jnp.float32)
            slabs.append(held[half * 3 * CH : (half + 1) * 3 * CH])
        for a in range(3):
            twisted = []
            for n in range(BLOCKS):
                part = slabs[n][a * CH : (a + 1) * CH]
                angle = math.pi * n / (2 * BLOCKS)
                twisted.append((part * math.cos(angle), part * -math.sin(angle)))
            for q, (re, im) in enumerate(dft(twisted, -1)):
                cos, sin = cos_ref[q : q + 1, :], sin_ref[q : q + 1, :]
                rows = pl.ds((q * 2 + half) * CH, CH)
                work[a, rows, :LANES] = re * cos + im * sin
                work[a, rows, LANES:] = im * cos - re * sin
    for a in range(3):
        spec[a] = product(work[a], mat_ref[0], mat_ref[1])
    step = 8 * CH
    for at in range(0, 2 * BLOCKS * CH, step):
        rows = pl.ds(at, step)
        tok_re, tok_im = spec[0, rows, :LANES], spec[0, rows, LANES:]
        grad_re, grad_im = spec[1, rows, :LANES], spec[1, rows, LANES:]
        filt_re, filt_im = spec[2, rows, :LANES], spec[2, rows, LANES:]
        swap = lambda x: jnp.concatenate(
            [x[(i ^ 1) * CH : (i ^ 1) * CH + CH] for i in range(step // CH)]
        )
        both_re = filt_re + swap(filt_re)
        both_im = filt_im - swap(filt_im)
        work[0, rows, :LANES] = both_re * tok_re - both_im * tok_im
        work[0, rows, LANES:] = both_re * tok_im + both_im * tok_re
        work[1, rows, :LANES] = both_re * grad_re + both_im * grad_im
        work[1, rows, LANES:] = both_re * grad_im - both_im * grad_re
    for a in range(2):
        spec[a] = product(work[a], mat_ref[2], mat_ref[3])
    for half in range(2):
        results = []
        for a in range(2):
            turned = []
            for q in range(BLOCKS):
                cos, sin = cos_ref[q : q + 1, :], sin_ref[q : q + 1, :]
                rows = pl.ds((q * 2 + half) * CH, CH)
                re, im = spec[a, rows, :LANES], spec[a, rows, LANES:]
                turned.append((re * cos - im * sin, re * sin + im * cos))
            made = []
            for n, (re, im) in enumerate(dft(turned, 1)):
                angle = math.pi * n / (2 * BLOCKS)
                scale = 2.0 / TOTAL
                made.append(re * (math.cos(angle) * scale) - im * (math.sin(angle) * scale))
            results.append(made)
        for n in range(BLOCKS):
            rows = pl.ds((n * 2 + half) * 2 * CH, 2 * CH)
            out_ref[rows, :] = jnp.concatenate([r[n] for r in results]).astype(jnp.bfloat16)


def body(tokens, cotangent, filters):
    cos, sin, matrices = tables()
    chans = tokens.shape[1]
    group = ("ctx", "half")
    vmem = pl.BlockSpec(memory_space=pltpu.VMEM)
    sent = pl.pallas_call(
        gather_kernel,
        out_shape=jax.ShapeDtypeStruct((3 * chans, LANES), jnp.bfloat16),
        in_specs=[vmem] * 3,
        out_specs=vmem,
        compiler_params=PARAMS,
    )(tokens, cotangent, filters)
    held = lax.all_to_all(sent, group, split_axis=0, concat_axis=0, tiled=True)
    made = pl.pallas_call(
        operator_kernel,
        out_shape=jax.ShapeDtypeStruct((2 * chans, LANES), jnp.bfloat16),
        in_specs=[vmem] * 4,
        out_specs=vmem,
        scratch_shapes=[
            pltpu.VMEM((3, 2 * BLOCKS * CH, 2 * LANES), jnp.float32),
            pltpu.VMEM((3, 2 * BLOCKS * CH, 2 * LANES), jnp.float32),
        ],
        compiler_params=PARAMS,
    )(held, cos, sin, matrices)
    back = lax.all_to_all(made, group, split_axis=0, concat_axis=0, tiled=True)
    return pl.pallas_call(
        scatter_kernel,
        out_shape=[jax.ShapeDtypeStruct((LANES, chans), jnp.bfloat16)] * 2,
        in_specs=[vmem],
        out_specs=[vmem] * 2,
        compiler_params=PARAMS,
    )(back)


def solution(mesh):
    halves = Mesh(mesh.devices.reshape(BLOCKS, 2, -1), ("ctx", "half", "rest"))
    placed = P("ctx", ("half", "rest"))
    return jax.shard_map(
        body,
        mesh=halves,
        in_specs=(placed,) * 3,
        out_specs=(placed,) * 2,
        check_vma=False,
    )
```

```python
import math

import jax
import jax.numpy as jnp
import numpy as np
from jax import lax
from jax.experimental import pallas as pl
from jax.experimental.pallas import tpu as pltpu
from jax.sharding import Mesh
from jax.sharding import PartitionSpec as P

LANES = 128
BLOCKS = 32
TOTAL = 2 * LANES * BLOCKS
CH = 8
PARAMS = pltpu.CompilerParams(vmem_limit_bytes=40 * 2**20)


def tables():
    q = np.arange(BLOCKS)[:, None]
    m = np.arange(LANES)[None, :]
    turn = 2.0 * math.pi * (2 * q + 0.5) * m / TOTAL
    lane = np.arange(LANES)
    phase = 2.0 * math.pi * (lane[:, None] * lane[None, :] % LANES) / LANES
    cos, sin = np.cos(phase), np.sin(phase)
    ahead = np.block([[cos, -sin], [sin, cos]]).astype(np.float32)
    halves = []
    for matrix in (ahead, ahead.T):
        high = matrix.astype(jnp.bfloat16)
        low = (matrix - high.astype(np.float32)).astype(jnp.bfloat16)
        halves += [high, low]
    return np.cos(turn).astype(np.float32), np.sin(turn).astype(np.float32), np.stack(halves)


def rotate(value, angle):
    re, im = value
    eighth = round(angle / (math.pi / 4), 9) % 8
    root = math.sqrt(0.5)
    if eighth == 0:
        return re, im
    if eighth == 2:
        return -im, re
    if eighth == 4:
        return -re, -im
    if eighth == 6:
        return im, -re
    if eighth in (1, 3, 5, 7):
        plus, minus = (re + im) * root, (re - im) * root
        return {1: (minus, plus), 3: (-plus, minus), 5: (-minus, -plus), 7: (plus, -minus)}[eighth]
    cos, sin = math.cos(angle), math.sin(angle)
    return re * cos - im * sin, re * sin + im * cos


def dft(values, sign):
    size = len(values)
    if size == 1:
        return values
    if size == 2:
        (ar, ai), (br, bi) = values
        return [(ar + br, ai + bi), (ar - br, ai - bi)]
    radix = 4
    if size % 4 or size == 8:
        radix = 2
    rest = size // radix
    parts = [dft(values[i::radix], sign) for i in range(radix)]
    out = [None] * size
    for k in range(rest):
        turned = [rotate(parts[i][k], sign * 2.0 * math.pi * i * k / size) for i in range(radix)]
        if radix == 2:
            (ar, ai), (br, bi) = turned
            out[k], out[k + rest] = (ar + br, ai + bi), (ar - br, ai - bi)
        else:
            (ar, ai), (br, bi), (cr, ci), (dr, di) = turned
            er, ei, fr, fi = ar + cr, ai + ci, ar - cr, ai - ci
            gr, gi, hr, hi = br + dr, bi + di, (br - dr) * sign, (bi - di) * sign
            out[k] = er + gr, ei + gi
            out[k + rest] = fr - hi, fi + hr
            out[k + 2 * rest] = er - gr, ei - gi
            out[k + 3 * rest] = fr + hi, fi - hr
    return out


def product(left, matrix_high, matrix_low):
    high = left.astype(jnp.bfloat16)
    low = (left - high.astype(jnp.float32)).astype(jnp.bfloat16)
    dot = lambda a, b: jnp.dot(a, b, preferred_element_type=jnp.float32)
    return dot(high, matrix_high) + (dot(low, matrix_high) + dot(high, matrix_low))


def gather_kernel(tok_hbm, grad_hbm, filt_hbm, out_ref, held, sems):
    copies = []
    for i, hbm in enumerate((tok_hbm, grad_hbm, filt_hbm)):
        copies.append(pltpu.make_async_copy(hbm, held.at[i], sems.at[i]))
        copies[-1].start()
    for copy in copies:
        copy.wait()
    for pair in range(out_ref.shape[0] // (6 * CH)):
        if pair % 8 == 0:
            cols = pl.ds(pair * 2 * CH, LANES)
            turned = [held[i, :, cols].astype(jnp.float32).T for i in range(3)]
        at = (pair % 8) * 2 * CH
        rows = [part[at + CH * i : at + CH * (i + 1)] for i in range(2) for part in turned]
        out_ref[pl.ds(pair * 6 * CH, 6 * CH), :] = jnp.concatenate(rows).astype(jnp.bfloat16)


def scatter_kernel(in_ref, out_hbm, grad_hbm, made, sems):
    rows = LANES // CH
    copies = []
    for i, hbm in enumerate((out_hbm, grad_hbm)):
        for block in range(hbm.shape[1] // LANES):
            held = in_ref[pl.ds(block * 2 * LANES, 2 * LANES), :].astype(jnp.float32)
            part = held.reshape(rows, 2, CH, LANES)[:, i].reshape(LANES, LANES).T
            made[i, :, pl.ds(block * LANES, LANES)] = part.astype(jnp.bfloat16)
        copies.append(pltpu.make_async_copy(made.at[i], hbm, sems.at[i]))
        copies[-1].start()
    for copy in copies:
        copy.wait()


def operator_kernel(in_ref, cos_ref, sin_ref, mat_ref, out_ref, work, spec):
    for half in range(2):
        slabs = []
        for n in range(BLOCKS):
            held = in_ref[pl.ds(n * 6 * CH, 6 * CH), :].astype(jnp.float32)
            slabs.append(held[half * 3 * CH : (half + 1) * 3 * CH])
        for a in range(3):
            twisted = []
            for n in range(BLOCKS):
                part = slabs[n][a * CH : (a + 1) * CH]
                angle = math.pi * n / (2 * BLOCKS)
                twisted.append((part * math.cos(angle), part * -math.sin(angle)))
            for q, (re, im) in enumerate(dft(twisted, -1)):
                cos, sin = cos_ref[q : q + 1, :], sin_ref[q : q + 1, :]
                rows = pl.ds((q * 2 + half) * CH, CH)
                work[a, rows, :LANES] = re * cos + im * sin
                work[a, rows, LANES:] = im * cos - re * sin
    for a in range(3):
        spec[a] = product(work[a], mat_ref[0], mat_ref[1])
    step = 8 * CH
    for at in range(0, 2 * BLOCKS * CH, step):
        rows = pl.ds(at, step)
        tok_re, tok_im = spec[0, rows, :LANES], spec[0, rows, LANES:]
        grad_re, grad_im = spec[1, rows, :LANES], spec[1, rows, LANES:]
        filt_re, filt_im = spec[2, rows, :LANES], spec[2, rows, LANES:]
        swap = lambda x: jnp.concatenate(
            [x[(i ^ 1) * CH : (i ^ 1) * CH + CH] for i in range(step // CH)]
        )
        both_re = filt_re + swap(filt_re)
        both_im = filt_im - swap(filt_im)
        work[0, rows, :LANES] = both_re * tok_re - both_im * tok_im
        work[0, rows, LANES:] = both_re * tok_im + both_im * tok_re
        work[1, rows, :LANES] = both_re * grad_re + both_im * grad_im
        work[1, rows, LANES:] = both_re * grad_im - both_im * grad_re
    for a in range(2):
        spec[a] = product(work[a], mat_ref[2], mat_ref[3])
    for half in range(2):
        results = []
        for a in range(2):
            turned = []
            for q in range(BLOCKS):
                cos, sin = cos_ref[q : q + 1, :], sin_ref[q : q + 1, :]
                rows = pl.ds((q * 2 + half) * CH, CH)
                re, im = spec[a, rows, :LANES], spec[a, rows, LANES:]
                turned.append((re * cos - im * sin, re * sin + im * cos))
            made = []
            for n, (re, im) in enumerate(dft(turned, 1)):
                angle = math.pi * n / (2 * BLOCKS)
                scale = 2.0 / TOTAL
                made.append(re * (math.cos(angle) * scale) - im * (math.sin(angle) * scale))
            results.append(made)
        for n in range(BLOCKS):
            rows = pl.ds((n * 2 + half) * 2 * CH, 2 * CH)
            out_ref[rows, :] = jnp.concatenate([r[n] for r in results]).astype(jnp.bfloat16)


def body(tokens, cotangent, filters):
    cos, sin, matrices = tables()
    chans = tokens.shape[1]
    group = ("ctx", "half")
    vmem = pl.BlockSpec(memory_space=pltpu.VMEM)
    hbm = pl.BlockSpec(memory_space=pltpu.HBM)
    fields = [pltpu.with_memory_space_constraint(x, pltpu.HBM) for x in (tokens, cotangent, filters)]
    sent = pl.pallas_call(
        gather_kernel,
        out_shape=pltpu.VMEM((3 * chans, LANES), jnp.bfloat16),
        in_specs=[hbm] * 3,
        out_specs=vmem,
        scratch_shapes=[pltpu.VMEM((3, LANES, chans), jnp.bfloat16), pltpu.SemaphoreType.DMA((3,))],
        compiler_params=PARAMS,
    )(*fields)
    held = lax.all_to_all(sent, group, split_axis=0, concat_axis=0, tiled=True)
    made = pl.pallas_call(
        operator_kernel,
        out_shape=pltpu.VMEM((2 * chans, LANES), jnp.bfloat16),
        in_specs=[vmem] * 4,
        out_specs=vmem,
        scratch_shapes=[
            pltpu.VMEM((3, 2 * BLOCKS * CH, 2 * LANES), jnp.float32),
            pltpu.VMEM((3, 2 * BLOCKS * CH, 2 * LANES), jnp.float32),
        ],
        compiler_params=PARAMS,
    )(held, cos, sin, matrices)
    back = lax.all_to_all(made, group, split_axis=0, concat_axis=0, tiled=True)
    return pl.pallas_call(
        scatter_kernel,
        out_shape=[jax.ShapeDtypeStruct((LANES, chans), jnp.bfloat16)] * 2,
        in_specs=[vmem],
        out_specs=[hbm] * 2,
        scratch_shapes=[pltpu.VMEM((2, LANES, chans), jnp.bfloat16), pltpu.SemaphoreType.DMA((2,))],
        compiler_params=PARAMS,
    )(back)


def solution(mesh):
    halves = Mesh(mesh.devices.reshape(BLOCKS, 2, -1), ("ctx", "half", "rest"))
    placed = P("ctx", ("half", "rest"))
    return jax.shard_map(
        body,
        mesh=halves,
        in_specs=(placed,) * 3,
        out_specs=(placed,) * 2,
        check_vma=False,
    )
```

```python
import math

import jax
import jax.numpy as jnp
import numpy as np
from jax import lax
from jax.experimental import pallas as pl
from jax.experimental.pallas import tpu as pltpu
from jax.sharding import PartitionSpec as P

LANES = 128
BLOCKS = 32
TOTAL = 2 * LANES * BLOCKS
CH = 8
PART = 128
PARAMS = pltpu.CompilerParams(vmem_limit_bytes=40 * 2**20)


def tables():
    q = np.arange(BLOCKS)[:, None]
    m = np.arange(LANES)[None, :]
    turn = 2.0 * math.pi * (2 * q + 0.5) * m / TOTAL
    lane = np.arange(LANES)
    phase = 2.0 * math.pi * (lane[:, None] * lane[None, :] % LANES) / LANES
    cos, sin = np.cos(phase), np.sin(phase)
    ahead = np.block([[cos, -sin], [sin, cos]]).astype(np.float32)
    halves = []
    for matrix in (ahead, ahead.T):
        high = matrix.astype(jnp.bfloat16)
        low = (matrix - high.astype(np.float32)).astype(jnp.bfloat16)
        halves.append(np.concatenate([high, high, low]))
    return np.cos(turn).astype(np.float32), np.sin(turn).astype(np.float32), np.stack(halves)


def rotate(value, angle):
    re, im = value
    eighth = round(angle / (math.pi / 4), 9) % 8
    root = math.sqrt(0.5)
    if eighth == 0:
        return re, im
    if eighth == 2:
        return -im, re
    if eighth == 4:
        return -re, -im
    if eighth == 6:
        return im, -re
    if eighth in (1, 3, 5, 7):
        plus, minus = (re + im) * root, (re - im) * root
        return {1: (minus, plus), 3: (-plus, minus), 5: (-minus, -plus), 7: (plus, -minus)}[eighth]
    cos, sin = math.cos(angle), math.sin(angle)
    return re * cos - im * sin, re * sin + im * cos


def dft(values, sign):
    size = len(values)
    if size == 1:
        return values
    if size == 2:
        (ar, ai), (br, bi) = values
        return [(ar + br, ai + bi), (ar - br, ai - bi)]
    radix = 4
    if size % 4 or size == 8:
        radix = 2
    rest = size // radix
    parts = [dft(values[i::radix], sign) for i in range(radix)]
    out = [None] * size
    for k in range(rest):
        turned = [rotate(parts[i][k], sign * 2.0 * math.pi * i * k / size) for i in range(radix)]
        if radix == 2:
            (ar, ai), (br, bi) = turned
            out[k], out[k + rest] = (ar + br, ai + bi), (ar - br, ai - bi)
        else:
            (ar, ai), (br, bi), (cr, ci), (dr, di) = turned
            er, ei, fr, fi = ar + cr, ai + ci, ar - cr, ai - ci
            gr, gi, hr, hi = br + dr, bi + di, (br - dr) * sign, (bi - di) * sign
            out[k] = er + gr, ei + gi
            out[k + rest] = fr - hi, fi + hr
            out[k + 2 * rest] = er - gr, ei - gi
            out[k + 3 * rest] = fr + hi, fi - hr
    return out


def product(left, matrix):
    high = left.astype(jnp.bfloat16)
    low = (left - high.astype(jnp.float32)).astype(jnp.bfloat16)
    parts = jnp.concatenate([high, low, high], axis=1)
    return jnp.dot(parts, matrix, preferred_element_type=jnp.float32)


def gather_kernel(tok_hbm, grad_hbm, filt_hbm, out_ref, held, sems):
    copies = []
    for i, hbm in enumerate((tok_hbm, grad_hbm, filt_hbm)):
        copies.append(pltpu.make_async_copy(hbm, held.at[i], sems.at[i]))
        copies[-1].start()
    for copy in copies:
        copy.wait()
    per = LANES // (2 * CH)
    for block in range(held.shape[2] // LANES):
        cols = pl.ds(block * LANES, LANES)
        turned = [held[i, :, cols].astype(jnp.float32).T for i in range(3)]
        for j in range(per):
            rows = [part[2 * CH * j : 2 * CH * (j + 1)] for part in turned]
            at = pl.ds((block * per + j) * 6 * CH, 6 * CH)
            out_ref[at, :] = jnp.concatenate(rows).astype(jnp.bfloat16)


def scatter_kernel(in_ref, out_hbm, grad_hbm, made, sems):
    rows = LANES // (2 * CH)
    copies = []
    for i, hbm in enumerate((out_hbm, grad_hbm)):
        for block in range(hbm.shape[1] // LANES):
            held = in_ref[pl.ds(block * 2 * LANES, 2 * LANES), :].astype(jnp.float32)
            part = held.reshape(rows, 2, 2 * CH, LANES)[:, i].reshape(LANES, LANES).T
            made[i, :, pl.ds(block * LANES, LANES)] = part.astype(jnp.bfloat16)
        copies.append(pltpu.make_async_copy(made.at[i], hbm, sems.at[i]))
        copies[-1].start()
    for copy in copies:
        copy.wait()


def mix(first, second):
    total = max(len(first), 1)
    done = 0
    for i, step in enumerate(first):
        step()
        while done < len(second) * (i + 1) // total:
            second[done]()
            done += 1
    for step in second[done:]:
        step()


def dft_steps(load, sign, store):
    parts = {}

    def inner(i):
        def step():
            parts[i] = dft([load(n) for n in range(i, BLOCKS, 4)], sign)
        return step

    def outer(k):
        def step():
            turned = [rotate(parts[i][k], sign * 2.0 * math.pi * i * k / BLOCKS) for i in range(4)]
            for j, value in enumerate(dft(turned, sign)):
                store(k + 8 * j, value)
        return step

    return [inner(i) for i in range(4)] + [outer(k) for k in range(8)]


def ahead(read, cos_ref, sin_ref, work, slab):
    def load(n):
        part, angle = read(n), math.pi * n / (2 * BLOCKS)
        return part * math.cos(angle), part * -math.sin(angle)

    def store(q, value):
        re, im = value
        cos, sin = cos_ref[q : q + 1, :], sin_ref[q : q + 1, :]
        rows = pl.ds((slab * BLOCKS + q) * CH, CH)
        work[rows, :LANES] = re * cos + im * sin
        work[rows, LANES:] = im * cos - re * sin

    return dft_steps(load, -1, store)


def lanes(work, spec, mat_ref, which, slab):
    def step(at):
        def run():
            rows = pl.ds(slab * BLOCKS * CH + at, PART)
            spec[rows] = product(work[rows], mat_ref[which])

        return run

    return [step(at) for at in range(0, BLOCKS * CH, PART)]


def field_kernel(in_ref, cos_ref, sin_ref, mat_ref, spec, work):
    def steps(a):
        made = []
        for slab in range(2):

            def read(n, slab=slab):
                held = in_ref[pl.ds(n * 6 * CH + a * 2 * CH, 2 * CH), :].astype(jnp.float32)
                return held[slab * CH : (slab + 1) * CH]

            made += ahead(read, cos_ref, sin_ref, work.at[a], slab)
        return made

    inner = lambda a: [s for h in range(2) for s in lanes(work.at[a], spec.at[a], mat_ref, 0, h)]
    mix(steps(0), [])
    mix(steps(1), inner(0))
    mix(steps(2), inner(1))
    mix([], inner(2))


def operator_kernel(in_ref, spec, cos_ref, sin_ref, mat_ref, out_ref, work, other):
    size = BLOCKS * CH

    def steps(slab):
        def read(n):
            held = in_ref[pl.ds(n * 2 * CH, 2 * CH), :].astype(jnp.float32)
            return held[slab * CH : (slab + 1) * CH]

        return ahead(read, cos_ref, sin_ref, work.at[2], slab)

    def multiply(slab):
        def step(at):
            def run():
                rows = pl.ds(slab * size + at, 64)
                re = spec[2, rows, :LANES] + other[2, rows, :LANES]
                im = spec[2, rows, LANES:] - other[2, rows, LANES:]
                for a, turn in enumerate((im, -im)):
                    has_re, has_im = spec[a, rows, :LANES], spec[a, rows, LANES:]
                    work[a, rows, :LANES] = re * has_re - turn * has_im
                    work[a, rows, LANES:] = re * has_im + turn * has_re

            return run

        return [step(at) for at in range(0, size, 64)]

    def back(a, slab):
        def load(q):
            cos, sin = cos_ref[q : q + 1, :], sin_ref[q : q + 1, :]
            rows = pl.ds(slab * size + q * CH, CH)
            re, im = other[a, rows, :LANES], other[a, rows, LANES:]
            return re * cos - im * sin, re * sin + im * cos

        def store(n, value):
            angle, scale = math.pi * n / (2 * BLOCKS), 2.0 / TOTAL
            re, im = value
            part = re * (math.cos(angle) * scale) - im * (math.sin(angle) * scale)
            kept = pl.ds(n * CH, CH)
            if slab == 0:
                work[2, kept, :LANES] = part
            else:
                both = jnp.concatenate([work[2, kept, :LANES], part])
                out_ref[pl.ds((n * 2 + a) * 2 * CH, 2 * CH), :] = both.astype(jnp.bfloat16)

        return dft_steps(load, 1, store)

    inner = lambda a, slab, which: lanes(work.at[a], other.at[a], mat_ref, which, slab)
    mix(steps(0), [])
    mix(steps(1), inner(2, 0, 0))
    mix(multiply(0), inner(2, 1, 0))
    mix(multiply(1), inner(0, 0, 1))
    mix(back(0, 0), inner(0, 1, 1))
    mix(back(0, 1), inner(1, 0, 1))
    mix(back(1, 0), inner(1, 1, 1))
    mix(back(1, 1), [])


def body(tokens, cotangent, filters):
    cos, sin, matrices = tables()
    chans = tokens.shape[1]
    rows = 2 * BLOCKS * CH
    mirror = lax.axis_size("tp") // 2
    vmem = pl.BlockSpec(memory_space=pltpu.VMEM)
    hbm = pl.BlockSpec(memory_space=pltpu.HBM)
    fields = [pltpu.with_memory_space_constraint(x, pltpu.HBM) for x in (tokens, cotangent, filters)]
    sent = pl.pallas_call(
        gather_kernel,
        out_shape=pltpu.VMEM((3 * chans, LANES), jnp.bfloat16),
        in_specs=[hbm] * 3,
        out_specs=vmem,
        scratch_shapes=[pltpu.VMEM((3, LANES, chans), jnp.bfloat16), pltpu.SemaphoreType.DMA((3,))],
        compiler_params=PARAMS,
    )(*fields)
    held = lax.all_to_all(sent, "ctx", split_axis=0, concat_axis=0, tiled=True)
    own = held.reshape(BLOCKS, 3, 2 * CH, LANES)[:, 2].reshape(rows, LANES)
    other = lax.ppermute(own, "tp", [(i, i ^ mirror) for i in range(2 * mirror)])
    spectra = pl.pallas_call(
        field_kernel,
        out_shape=pltpu.VMEM((3, rows, 2 * LANES), jnp.float32),
        in_specs=[vmem] * 4,
        out_specs=vmem,
        scratch_shapes=[pltpu.VMEM((3, rows, 2 * LANES), jnp.float32)],
        compiler_params=PARAMS,
        cost_estimate=pl.CostEstimate(flops=10**9, bytes_accessed=10**6, transcendentals=0),
    )(held, cos, sin, matrices)
    made = pl.pallas_call(
        operator_kernel,
        out_shape=pltpu.VMEM((2 * chans, LANES), jnp.bfloat16),
        in_specs=[vmem] * 5,
        out_specs=vmem,
        scratch_shapes=[pltpu.VMEM((3, rows, 2 * LANES), jnp.float32)] * 2,
        compiler_params=PARAMS,
        cost_estimate=pl.CostEstimate(flops=10**9, bytes_accessed=10**6, transcendentals=0),
    )(other, spectra, cos, sin, matrices)
    back = lax.all_to_all(made, "ctx", split_axis=0, concat_axis=0, tiled=True)
    return pl.pallas_call(
        scatter_kernel,
        out_shape=[jax.ShapeDtypeStruct((LANES, chans), jnp.bfloat16)] * 2,
        in_specs=[vmem],
        out_specs=[hbm] * 2,
        scratch_shapes=[pltpu.VMEM((2, LANES, chans), jnp.bfloat16), pltpu.SemaphoreType.DMA((2,))],
        compiler_params=PARAMS,
    )(back)


def solution(mesh):
    return jax.shard_map(
        body,
        mesh=mesh,
        in_specs=(P("ctx", "tp"),) * 3,
        out_specs=(P("ctx", "tp"),) * 2,
        check_vma=False,
    )
```

```python
import math

import jax
import jax.numpy as jnp
import numpy as np
from jax import lax
from jax.experimental import pallas as pl
from jax.experimental.pallas import tpu as pltpu
from jax.sharding import PartitionSpec as P

LANES = 128
BLOCKS = 32
TOTAL = 2 * LANES * BLOCKS
CH = 8
PART = 128
ORDER = (4, 12, 24, 2, 28, 10, 18, 27, 21, 9, 19, 8, 6, 17, 13, 15, 29, 3, 5, 1, 7, 14, 0, 31, 20, 30, 26, 22, 25, 11, 23, 16)
PLACE = tuple(ORDER.index(n) for n in range(BLOCKS))
PARAMS = pltpu.CompilerParams(vmem_limit_bytes=40 * 2**20)


def tables():
    q = np.arange(BLOCKS)[:, None]
    m = np.arange(LANES)[None, :]
    turn = 2.0 * math.pi * (2 * q + 0.5) * m / TOTAL
    lane = np.arange(LANES)
    phase = 2.0 * math.pi * (lane[:, None] * lane[None, :] % LANES) / LANES
    cos, sin = np.cos(phase), np.sin(phase)
    ahead = np.block([[cos, -sin], [sin, cos]]).astype(np.float32)
    halves = []
    for matrix in (ahead, ahead.T):
        high = matrix.astype(jnp.bfloat16)
        low = (matrix - high.astype(np.float32)).astype(jnp.bfloat16)
        halves.append(np.concatenate([high, high, low]))
    return np.cos(turn).astype(np.float32), np.sin(turn).astype(np.float32), np.stack(halves)


def rotate(value, angle):
    re, im = value
    eighth = round(angle / (math.pi / 4), 9) % 8
    root = math.sqrt(0.5)
    if eighth == 0:
        return re, im
    if eighth == 2:
        return -im, re
    if eighth == 4:
        return -re, -im
    if eighth == 6:
        return im, -re
    if eighth in (1, 3, 5, 7):
        plus, minus = (re + im) * root, (re - im) * root
        return {1: (minus, plus), 3: (-plus, minus), 5: (-minus, -plus), 7: (plus, -minus)}[eighth]
    cos, sin = math.cos(angle), math.sin(angle)
    return re * cos - im * sin, re * sin + im * cos


def dft(values, sign):
    size = len(values)
    if size == 1:
        return values
    if size == 2:
        (ar, ai), (br, bi) = values
        return [(ar + br, ai + bi), (ar - br, ai - bi)]
    radix = 4
    if size % 4 or size == 8:
        radix = 2
    rest = size // radix
    parts = [dft(values[i::radix], sign) for i in range(radix)]
    out = [None] * size
    for k in range(rest):
        turned = [rotate(parts[i][k], sign * 2.0 * math.pi * i * k / size) for i in range(radix)]
        if radix == 2:
            (ar, ai), (br, bi) = turned
            out[k], out[k + rest] = (ar + br, ai + bi), (ar - br, ai - bi)
        else:
            (ar, ai), (br, bi), (cr, ci), (dr, di) = turned
            er, ei, fr, fi = ar + cr, ai + ci, ar - cr, ai - ci
            gr, gi, hr, hi = br + dr, bi + di, (br - dr) * sign, (bi - di) * sign
            out[k] = er + gr, ei + gi
            out[k + rest] = fr - hi, fi + hr
            out[k + 2 * rest] = er - gr, ei - gi
            out[k + 3 * rest] = fr + hi, fi - hr
    return out


def product(left, matrix):
    high = left.astype(jnp.bfloat16)
    low = (left - high.astype(jnp.float32)).astype(jnp.bfloat16)
    parts = jnp.concatenate([high, low, high], axis=1)
    return jnp.dot(parts, matrix, preferred_element_type=jnp.float32)


def gather_kernel(tok_hbm, grad_hbm, filt_hbm, out_ref, held, sems):
    copies = []
    for i, hbm in enumerate((tok_hbm, grad_hbm, filt_hbm)):
        copies.append(pltpu.make_async_copy(hbm, held.at[i], sems.at[i]))
        copies[-1].start()
    for copy in copies:
        copy.wait()
    per = LANES // (2 * CH)
    for block in range(held.shape[2] // LANES):
        cols = pl.ds(block * LANES, LANES)
        turned = [held[i, :, cols].astype(jnp.float32).T for i in range(3)]
        for j in range(per):
            rows = [part[2 * CH * j : 2 * CH * (j + 1)] for part in turned]
            at = pl.ds(PLACE[block * per + j] * 6 * CH, 6 * CH)
            out_ref[at, :] = jnp.concatenate(rows).astype(jnp.bfloat16)


def scatter_kernel(in_ref, out_hbm, grad_hbm, made, sems):
    rows = LANES // (2 * CH)
    copies = []
    for i, hbm in enumerate((out_hbm, grad_hbm)):
        for block in range(hbm.shape[1] // LANES):
            spots = [(PLACE[block * rows + j] * 2 + i) * 2 * CH for j in range(rows)]
            held = [in_ref[pl.ds(at, 2 * CH), :].astype(jnp.float32) for at in spots]
            part = jnp.concatenate(held).T
            made[i, :, pl.ds(block * LANES, LANES)] = part.astype(jnp.bfloat16)
        copies.append(pltpu.make_async_copy(made.at[i], hbm, sems.at[i]))
        copies[-1].start()
    for copy in copies:
        copy.wait()


def mix(first, second):
    total = max(len(first), 1)
    done = 0
    for i, step in enumerate(first):
        step()
        while done < len(second) * (i + 1) // total:
            second[done]()
            done += 1
    for step in second[done:]:
        step()


def dft_steps(load, sign, store):
    parts = {}

    def inner(i):
        def step():
            parts[i] = dft([load(n) for n in range(i, BLOCKS, 4)], sign)
        return step

    def outer(k):
        def step():
            turned = [rotate(parts[i][k], sign * 2.0 * math.pi * i * k / BLOCKS) for i in range(4)]
            for j, value in enumerate(dft(turned, sign)):
                store(k + 8 * j, value)
        return step

    return [inner(i) for i in range(4)] + [outer(k) for k in range(8)]


def ahead(read, cos_ref, sin_ref, work, slab):
    def load(n):
        part, angle = read(n), math.pi * n / (2 * BLOCKS)
        return part * math.cos(angle), part * -math.sin(angle)

    def store(q, value):
        re, im = value
        cos, sin = cos_ref[q : q + 1, :], sin_ref[q : q + 1, :]
        rows = pl.ds((slab * BLOCKS + q) * CH, CH)
        work[rows, :LANES] = re * cos + im * sin
        work[rows, LANES:] = im * cos - re * sin

    return dft_steps(load, -1, store)


def lanes(work, spec, mat_ref, which, slab):
    def step(at):
        def run():
            rows = pl.ds(slab * BLOCKS * CH + at, PART)
            spec[rows] = product(work[rows], mat_ref[which])

        return run

    return [step(at) for at in range(0, BLOCKS * CH, PART)]


def field_kernel(in_ref, cos_ref, sin_ref, mat_ref, spec, work):
    def steps(a):
        made = []
        for slab in range(2):

            def read(n, slab=slab):
                held = in_ref[pl.ds((PLACE[n] * 3 + a) * 2 * CH, 2 * CH), :].astype(jnp.float32)
                return held[slab * CH : (slab + 1) * CH]

            made += ahead(read, cos_ref, sin_ref, work.at[a], slab)
        return made

    inner = lambda a: [s for h in range(2) for s in lanes(work.at[a], spec.at[a], mat_ref, 0, h)]
    mix(steps(0), [])
    mix(steps(1), inner(0))
    mix(steps(2), inner(1))
    mix([], inner(2))


def operator_kernel(in_ref, spec, cos_ref, sin_ref, mat_ref, out_ref, work, other):
    size = BLOCKS * CH

    def steps(slab):
        def read(n):
            held = in_ref[pl.ds(PLACE[n] * 2 * CH, 2 * CH), :].astype(jnp.float32)
            return held[slab * CH : (slab + 1) * CH]

        return ahead(read, cos_ref, sin_ref, work.at[2], slab)

    def multiply(slab):
        def step(at):
            def run():
                rows = pl.ds(slab * size + at, 64)
                re = spec[2, rows, :LANES] + other[2, rows, :LANES]
                im = spec[2, rows, LANES:] - other[2, rows, LANES:]
                for a, turn in enumerate((im, -im)):
                    has_re, has_im = spec[a, rows, :LANES], spec[a, rows, LANES:]
                    work[a, rows, :LANES] = re * has_re - turn * has_im
                    work[a, rows, LANES:] = re * has_im + turn * has_re

            return run

        return [step(at) for at in range(0, size, 64)]

    def back(a, slab):
        def load(q):
            cos, sin = cos_ref[q : q + 1, :], sin_ref[q : q + 1, :]
            rows = pl.ds(slab * size + q * CH, CH)
            re, im = other[a, rows, :LANES], other[a, rows, LANES:]
            return re * cos - im * sin, re * sin + im * cos

        def store(n, value):
            angle, scale = math.pi * n / (2 * BLOCKS), 2.0 / TOTAL
            re, im = value
            part = re * (math.cos(angle) * scale) - im * (math.sin(angle) * scale)
            kept = pl.ds(n * CH, CH)
            if slab == 0:
                work[2, kept, :LANES] = part
            else:
                both = jnp.concatenate([work[2, kept, :LANES], part])
                out_ref[pl.ds((PLACE[n] * 2 + a) * 2 * CH, 2 * CH), :] = both.astype(jnp.bfloat16)

        return dft_steps(load, 1, store)

    inner = lambda a, slab, which: lanes(work.at[a], other.at[a], mat_ref, which, slab)
    mix(steps(0), [])
    mix(steps(1), inner(2, 0, 0))
    mix(multiply(0), inner(2, 1, 0))
    mix(multiply(1), inner(0, 0, 1))
    mix(back(0, 0), inner(0, 1, 1))
    mix(back(0, 1), inner(1, 0, 1))
    mix(back(1, 0), inner(1, 1, 1))
    mix(back(1, 1), [])


def exchange(rows):
    return lax.all_to_all(
        rows, "ctx", split_axis=0, concat_axis=0, tiled=True, axis_index_groups=[list(ORDER)]
    )


def body(tokens, cotangent, filters):
    cos, sin, matrices = tables()
    chans = tokens.shape[1]
    rows = 2 * BLOCKS * CH
    mirror = lax.axis_size("tp") // 2
    vmem = pl.BlockSpec(memory_space=pltpu.VMEM)
    hbm = pl.BlockSpec(memory_space=pltpu.HBM)
    fields = [pltpu.with_memory_space_constraint(x, pltpu.HBM) for x in (tokens, cotangent, filters)]
    sent = pl.pallas_call(
        gather_kernel,
        out_shape=pltpu.VMEM((3 * chans, LANES), jnp.bfloat16),
        in_specs=[hbm] * 3,
        out_specs=vmem,
        scratch_shapes=[pltpu.VMEM((3, LANES, chans), jnp.bfloat16), pltpu.SemaphoreType.DMA((3,))],
        compiler_params=PARAMS,
    )(*fields)
    held = exchange(sent)
    own = held.reshape(BLOCKS, 3, 2 * CH, LANES)[:, 2].reshape(rows, LANES)
    other = lax.ppermute(own, "tp", [(i, i ^ mirror) for i in range(2 * mirror)])
    spectra = pl.pallas_call(
        field_kernel,
        out_shape=pltpu.VMEM((3, rows, 2 * LANES), jnp.float32),
        in_specs=[vmem] * 4,
        out_specs=vmem,
        scratch_shapes=[pltpu.VMEM((3, rows, 2 * LANES), jnp.float32)],
        compiler_params=PARAMS,
        cost_estimate=pl.CostEstimate(flops=10**9, bytes_accessed=10**6, transcendentals=0),
    )(held, cos, sin, matrices)
    made = pl.pallas_call(
        operator_kernel,
        out_shape=pltpu.VMEM((2 * chans, LANES), jnp.bfloat16),
        in_specs=[vmem] * 5,
        out_specs=vmem,
        scratch_shapes=[pltpu.VMEM((3, rows, 2 * LANES), jnp.float32)] * 2,
        compiler_params=PARAMS,
        cost_estimate=pl.CostEstimate(flops=10**9, bytes_accessed=10**6, transcendentals=0),
    )(other, spectra, cos, sin, matrices)
    back = exchange(made)
    return pl.pallas_call(
        scatter_kernel,
        out_shape=[jax.ShapeDtypeStruct((LANES, chans), jnp.bfloat16)] * 2,
        in_specs=[vmem],
        out_specs=[hbm] * 2,
        scratch_shapes=[pltpu.VMEM((2, LANES, chans), jnp.bfloat16), pltpu.SemaphoreType.DMA((2,))],
        compiler_params=PARAMS,
    )(back)


def solution(mesh):
    return jax.shard_map(
        body,
        mesh=mesh,
        in_specs=(P("ctx", "tp"),) * 3,
        out_specs=(P("ctx", "tp"),) * 2,
        check_vma=False,
    )
```

```python
import math

import jax
import jax.numpy as jnp
import numpy as np
from jax import lax
from jax.experimental import pallas as pl
from jax.experimental.pallas import tpu as pltpu
from jax.sharding import PartitionSpec as P

LANES = 128
BLOCKS = 32
TOTAL = 2 * LANES * BLOCKS
CH = 8
PART = 128
ORDER_IN = (28, 9, 19, 10, 29, 5, 7, 22, 0, 14, 8, 15, 23, 24, 21, 13, 25, 27, 6, 16, 26, 18, 11, 3, 17, 2, 1, 31, 12, 4, 30, 20)
ORDER_OUT = (4, 12, 24, 2, 28, 10, 18, 27, 21, 9, 19, 8, 6, 17, 13, 15, 29, 3, 5, 1, 7, 14, 0, 31, 20, 30, 26, 22, 25, 11, 23, 16)
PLACE_IN = tuple(ORDER_IN.index(n) for n in range(BLOCKS))
PLACE_OUT = tuple(ORDER_OUT.index(n) for n in range(BLOCKS))
PARAMS = pltpu.CompilerParams(vmem_limit_bytes=40 * 2**20)


def tables():
    q = np.arange(BLOCKS)[:, None]
    m = np.arange(LANES)[None, :]
    turn = 2.0 * math.pi * (2 * q + 0.5) * m / TOTAL
    lane = np.arange(LANES)
    phase = 2.0 * math.pi * (lane[:, None] * lane[None, :] % LANES) / LANES
    cos, sin = np.cos(phase), np.sin(phase)
    ahead = np.block([[cos, -sin], [sin, cos]]).astype(np.float32)
    halves = []
    for matrix in (ahead, ahead.T):
        high = matrix.astype(jnp.bfloat16)
        low = (matrix - high.astype(np.float32)).astype(jnp.bfloat16)
        halves.append(np.concatenate([high, high, low]))
    return np.cos(turn).astype(np.float32), np.sin(turn).astype(np.float32), np.stack(halves)


def rotate(value, angle):
    re, im = value
    eighth = round(angle / (math.pi / 4), 9) % 8
    root = math.sqrt(0.5)
    if eighth == 0:
        return re, im
    if eighth == 2:
        return -im, re
    if eighth == 4:
        return -re, -im
    if eighth == 6:
        return im, -re
    if eighth in (1, 3, 5, 7):
        plus, minus = (re + im) * root, (re - im) * root
        return {1: (minus, plus), 3: (-plus, minus), 5: (-minus, -plus), 7: (plus, -minus)}[eighth]
    cos, sin = math.cos(angle), math.sin(angle)
    return re * cos - im * sin, re * sin + im * cos


def dft(values, sign):
    size = len(values)
    if size == 1:
        return values
    if size == 2:
        (ar, ai), (br, bi) = values
        return [(ar + br, ai + bi), (ar - br, ai - bi)]
    radix = 4
    if size % 4 or size == 8:
        radix = 2
    rest = size // radix
    parts = [dft(values[i::radix], sign) for i in range(radix)]
    out = [None] * size
    for k in range(rest):
        turned = [rotate(parts[i][k], sign * 2.0 * math.pi * i * k / size) for i in range(radix)]
        if radix == 2:
            (ar, ai), (br, bi) = turned
            out[k], out[k + rest] = (ar + br, ai + bi), (ar - br, ai - bi)
        else:
            (ar, ai), (br, bi), (cr, ci), (dr, di) = turned
            er, ei, fr, fi = ar + cr, ai + ci, ar - cr, ai - ci
            gr, gi, hr, hi = br + dr, bi + di, (br - dr) * sign, (bi - di) * sign
            out[k] = er + gr, ei + gi
            out[k + rest] = fr - hi, fi + hr
            out[k + 2 * rest] = er - gr, ei - gi
            out[k + 3 * rest] = fr + hi, fi - hr
    return out


def product(left, matrix):
    high = left.astype(jnp.bfloat16)
    low = (left - high.astype(jnp.float32)).astype(jnp.bfloat16)
    parts = jnp.concatenate([high, low, high], axis=1)
    return jnp.dot(parts, matrix, preferred_element_type=jnp.float32)


def gather_kernel(tok_hbm, grad_hbm, filt_hbm, out_ref, held, sems):
    copies = []
    for i, hbm in enumerate((tok_hbm, grad_hbm, filt_hbm)):
        copies.append(pltpu.make_async_copy(hbm, held.at[i], sems.at[i]))
        copies[-1].start()
    for copy in copies:
        copy.wait()
    per = LANES // (2 * CH)
    for block in range(held.shape[2] // LANES):
        cols = pl.ds(block * LANES, LANES)
        turned = [held[i, :, cols].astype(jnp.float32).T for i in range(3)]
        for j in range(per):
            rows = [part[2 * CH * j : 2 * CH * (j + 1)] for part in turned]
            at = pl.ds(PLACE_IN[block * per + j] * 6 * CH, 6 * CH)
            out_ref[at, :] = jnp.concatenate(rows).astype(jnp.bfloat16)


def scatter_kernel(in_ref, out_hbm, grad_hbm, made, sems):
    rows = LANES // (2 * CH)
    copies = []
    for i, hbm in enumerate((out_hbm, grad_hbm)):
        for block in range(hbm.shape[1] // LANES):
            spots = [(PLACE_OUT[block * rows + j] * 2 + i) * 2 * CH for j in range(rows)]
            held = [in_ref[pl.ds(at, 2 * CH), :].astype(jnp.float32) for at in spots]
            part = jnp.concatenate(held).T
            made[i, :, pl.ds(block * LANES, LANES)] = part.astype(jnp.bfloat16)
        copies.append(pltpu.make_async_copy(made.at[i], hbm, sems.at[i]))
        copies[-1].start()
    for copy in copies:
        copy.wait()


def mix(first, second):
    total = max(len(first), 1)
    done = 0
    for i, step in enumerate(first):
        step()
        while done < len(second) * (i + 1) // total:
            second[done]()
            done += 1
    for step in second[done:]:
        step()


def dft_steps(load, sign, store):
    parts = {}

    def inner(i):
        def step():
            parts[i] = dft([load(n) for n in range(i, BLOCKS, 4)], sign)
        return step

    def outer(k):
        def step():
            turned = [rotate(parts[i][k], sign * 2.0 * math.pi * i * k / BLOCKS) for i in range(4)]
            for j, value in enumerate(dft(turned, sign)):
                store(k + 8 * j, value)
        return step

    return [inner(i) for i in range(4)] + [outer(k) for k in range(8)]


def ahead(read, cos_ref, sin_ref, work, slab):
    def load(n):
        part, angle = read(n), math.pi * n / (2 * BLOCKS)
        return part * math.cos(angle), part * -math.sin(angle)

    def store(q, value):
        re, im = value
        cos, sin = cos_ref[q : q + 1, :], sin_ref[q : q + 1, :]
        rows = pl.ds((slab * BLOCKS + q) * CH, CH)
        work[rows, :LANES] = re * cos + im * sin
        work[rows, LANES:] = im * cos - re * sin

    return dft_steps(load, -1, store)


def lanes(work, spec, mat_ref, which, slab):
    def step(at):
        def run():
            rows = pl.ds(slab * BLOCKS * CH + at, PART)
            spec[rows] = product(work[rows], mat_ref[which])

        return run

    return [step(at) for at in range(0, BLOCKS * CH, PART)]


def field_kernel(in_ref, cos_ref, sin_ref, mat_ref, spec, work):
    def steps(a):
        made = []
        for slab in range(2):

            def read(n, slab=slab):
                held = in_ref[pl.ds((PLACE_IN[n] * 3 + a) * 2 * CH, 2 * CH), :].astype(jnp.float32)
                return held[slab * CH : (slab + 1) * CH]

            made += ahead(read, cos_ref, sin_ref, work.at[a], slab)
        return made

    inner = lambda a: [s for h in range(2) for s in lanes(work.at[a], spec.at[a], mat_ref, 0, h)]
    mix(steps(0), [])
    mix(steps(1), inner(0))
    mix(steps(2), inner(1))
    mix([], inner(2))


def operator_kernel(in_ref, spec, cos_ref, sin_ref, mat_ref, out_ref, work, other):
    size = BLOCKS * CH

    def steps(slab):
        def read(n):
            held = in_ref[pl.ds(PLACE_IN[n] * 2 * CH, 2 * CH), :].astype(jnp.float32)
            return held[slab * CH : (slab + 1) * CH]

        return ahead(read, cos_ref, sin_ref, work.at[2], slab)

    def multiply(slab):
        def step(at):
            def run():
                rows = pl.ds(slab * size + at, 64)
                re = spec[2, rows, :LANES] + other[2, rows, :LANES]
                im = spec[2, rows, LANES:] - other[2, rows, LANES:]
                for a, turn in enumerate((im, -im)):
                    has_re, has_im = spec[a, rows, :LANES], spec[a, rows, LANES:]
                    work[a, rows, :LANES] = re * has_re - turn * has_im
                    work[a, rows, LANES:] = re * has_im + turn * has_re

            return run

        return [step(at) for at in range(0, size, 64)]

    def back(a, slab):
        def load(q):
            cos, sin = cos_ref[q : q + 1, :], sin_ref[q : q + 1, :]
            rows = pl.ds(slab * size + q * CH, CH)
            re, im = other[a, rows, :LANES], other[a, rows, LANES:]
            return re * cos - im * sin, re * sin + im * cos

        def store(n, value):
            angle, scale = math.pi * n / (2 * BLOCKS), 2.0 / TOTAL
            re, im = value
            part = re * (math.cos(angle) * scale) - im * (math.sin(angle) * scale)
            kept = pl.ds(n * CH, CH)
            if slab == 0:
                work[2, kept, :LANES] = part
            else:
                both = jnp.concatenate([work[2, kept, :LANES], part])
                out_ref[pl.ds((PLACE_OUT[n] * 2 + a) * 2 * CH, 2 * CH), :] = both.astype(jnp.bfloat16)

        return dft_steps(load, 1, store)

    inner = lambda a, slab, which: lanes(work.at[a], other.at[a], mat_ref, which, slab)
    mix(steps(0), [])
    mix(steps(1), inner(2, 0, 0))
    mix(multiply(0), inner(2, 1, 0))
    mix(multiply(1), inner(0, 0, 1))
    mix(back(0, 0), inner(0, 1, 1))
    mix(back(0, 1), inner(1, 0, 1))
    mix(back(1, 0), inner(1, 1, 1))
    mix(back(1, 1), [])


def exchange(rows, order):
    return lax.all_to_all(
        rows, "ctx", split_axis=0, concat_axis=0, tiled=True, axis_index_groups=[list(order)]
    )


def body(tokens, cotangent, filters):
    cos, sin, matrices = tables()
    chans = tokens.shape[1]
    rows = 2 * BLOCKS * CH
    mirror = lax.axis_size("tp") // 2
    vmem = pl.BlockSpec(memory_space=pltpu.VMEM)
    hbm = pl.BlockSpec(memory_space=pltpu.HBM)
    fields = [pltpu.with_memory_space_constraint(x, pltpu.HBM) for x in (tokens, cotangent, filters)]
    sent = pl.pallas_call(
        gather_kernel,
        out_shape=pltpu.VMEM((3 * chans, LANES), jnp.bfloat16),
        in_specs=[hbm] * 3,
        out_specs=vmem,
        scratch_shapes=[pltpu.VMEM((3, LANES, chans), jnp.bfloat16), pltpu.SemaphoreType.DMA((3,))],
        compiler_params=PARAMS,
    )(*fields)
    held = exchange(sent, ORDER_IN)
    own = held.reshape(BLOCKS, 3, 2 * CH, LANES)[:, 2].reshape(rows, LANES)
    other = lax.ppermute(own, "tp", [(i, i ^ mirror) for i in range(2 * mirror)])
    spectra = pl.pallas_call(
        field_kernel,
        out_shape=pltpu.VMEM((3, rows, 2 * LANES), jnp.float32),
        in_specs=[vmem] * 4,
        out_specs=vmem,
        scratch_shapes=[pltpu.VMEM((3, rows, 2 * LANES), jnp.float32)],
        compiler_params=PARAMS,
        cost_estimate=pl.CostEstimate(flops=10**9, bytes_accessed=10**6, transcendentals=0),
    )(held, cos, sin, matrices)
    made = pl.pallas_call(
        operator_kernel,
        out_shape=pltpu.VMEM((2 * chans, LANES), jnp.bfloat16),
        in_specs=[vmem] * 5,
        out_specs=vmem,
        scratch_shapes=[pltpu.VMEM((3, rows, 2 * LANES), jnp.float32)] * 2,
        compiler_params=PARAMS,
        cost_estimate=pl.CostEstimate(flops=10**9, bytes_accessed=10**6, transcendentals=0),
    )(other, spectra, cos, sin, matrices)
    back = exchange(made, ORDER_OUT)
    return pl.pallas_call(
        scatter_kernel,
        out_shape=[jax.ShapeDtypeStruct((LANES, chans), jnp.bfloat16)] * 2,
        in_specs=[vmem],
        out_specs=[hbm] * 2,
        scratch_shapes=[pltpu.VMEM((2, LANES, chans), jnp.bfloat16), pltpu.SemaphoreType.DMA((2,))],
        compiler_params=PARAMS,
    )(back)


def solution(mesh):
    return jax.shard_map(
        body,
        mesh=mesh,
        in_specs=(P("ctx", "tp"),) * 3,
        out_specs=(P("ctx", "tp"),) * 2,
        check_vma=False,
    )
```

```python
import math

import jax
import jax.numpy as jnp
import numpy as np
from jax import lax
from jax.experimental import pallas as pl
from jax.experimental.pallas import tpu as pltpu
from jax.sharding import PartitionSpec as P

LANES = 128
BLOCKS = 32
TOTAL = 2 * LANES * BLOCKS
CH = 8
PART = 128
ORDER_IN = (29, 26, 10, 14, 23, 16, 17, 11, 24, 13, 20, 15, 22, 2, 7, 6, 30, 9, 19, 21, 28, 25, 18, 5, 0, 1, 27, 31, 12, 8, 3, 4)
ORDER_OUT = (4, 12, 24, 2, 28, 10, 18, 27, 21, 9, 19, 8, 6, 17, 13, 15, 29, 3, 5, 1, 7, 14, 0, 31, 20, 30, 26, 22, 25, 11, 23, 16)
PLACE_IN = tuple(ORDER_IN.index(n) for n in range(BLOCKS))
PLACE_OUT = tuple(ORDER_OUT.index(n) for n in range(BLOCKS))
PARAMS = pltpu.CompilerParams(vmem_limit_bytes=40 * 2**20)


def tables():
    q = np.arange(BLOCKS)[:, None]
    m = np.arange(LANES)[None, :]
    turn = 2.0 * math.pi * (2 * q + 0.5) * m / TOTAL
    lane = np.arange(LANES)
    phase = 2.0 * math.pi * (lane[:, None] * lane[None, :] % LANES) / LANES
    cos, sin = np.cos(phase), np.sin(phase)
    ahead = np.block([[cos, -sin], [sin, cos]]).astype(np.float32)
    halves = []
    for matrix in (ahead, ahead.T):
        high = matrix.astype(jnp.bfloat16)
        low = (matrix - high.astype(np.float32)).astype(jnp.bfloat16)
        halves.append(np.concatenate([high, high, low]))
    return np.cos(turn).astype(np.float32), np.sin(turn).astype(np.float32), np.stack(halves)


def rotate(value, angle):
    re, im = value
    eighth = round(angle / (math.pi / 4), 9) % 8
    root = math.sqrt(0.5)
    if eighth == 0:
        return re, im
    if eighth == 2:
        return -im, re
    if eighth == 4:
        return -re, -im
    if eighth == 6:
        return im, -re
    if eighth in (1, 3, 5, 7):
        plus, minus = (re + im) * root, (re - im) * root
        return {1: (minus, plus), 3: (-plus, minus), 5: (-minus, -plus), 7: (plus, -minus)}[eighth]
    cos, sin = math.cos(angle), math.sin(angle)
    return re * cos - im * sin, re * sin + im * cos


def dft(values, sign):
    size = len(values)
    if size == 1:
        return values
    if size == 2:
        (ar, ai), (br, bi) = values
        return [(ar + br, ai + bi), (ar - br, ai - bi)]
    radix = 4
    if size % 4 or size == 8:
        radix = 2
    rest = size // radix
    parts = [dft(values[i::radix], sign) for i in range(radix)]
    out = [None] * size
    for k in range(rest):
        turned = [rotate(parts[i][k], sign * 2.0 * math.pi * i * k / size) for i in range(radix)]
        if radix == 2:
            (ar, ai), (br, bi) = turned
            out[k], out[k + rest] = (ar + br, ai + bi), (ar - br, ai - bi)
        else:
            (ar, ai), (br, bi), (cr, ci), (dr, di) = turned
            er, ei, fr, fi = ar + cr, ai + ci, ar - cr, ai - ci
            gr, gi, hr, hi = br + dr, bi + di, (br - dr) * sign, (bi - di) * sign
            out[k] = er + gr, ei + gi
            out[k + rest] = fr - hi, fi + hr
            out[k + 2 * rest] = er - gr, ei - gi
            out[k + 3 * rest] = fr + hi, fi - hr
    return out


def product(left, matrix):
    high = left.astype(jnp.bfloat16)
    low = (left - high.astype(jnp.float32)).astype(jnp.bfloat16)
    parts = jnp.concatenate([high, low, high], axis=1)
    return jnp.dot(parts, matrix, preferred_element_type=jnp.float32)


def gather_kernel(tok_hbm, grad_hbm, filt_hbm, out_ref, held, sems):
    copies = []
    for i, hbm in enumerate((tok_hbm, grad_hbm, filt_hbm)):
        copies.append(pltpu.make_async_copy(hbm, held.at[i], sems.at[i]))
        copies[-1].start()
    for copy in copies:
        copy.wait()
    per = LANES // (2 * CH)
    for block in range(held.shape[2] // LANES):
        cols = pl.ds(block * LANES, LANES)
        turned = [held[i, :, cols].astype(jnp.float32).T for i in range(3)]
        for j in range(per):
            rows = [part[2 * CH * j : 2 * CH * (j + 1)] for part in turned]
            at = pl.ds(PLACE_IN[block * per + j] * 6 * CH, 6 * CH)
            out_ref[at, :] = jnp.concatenate(rows).astype(jnp.bfloat16)


def scatter_kernel(in_ref, out_hbm, grad_hbm, made, sems):
    rows = LANES // (2 * CH)
    copies = []
    for i, hbm in enumerate((out_hbm, grad_hbm)):
        for block in range(hbm.shape[1] // LANES):
            spots = [(PLACE_OUT[block * rows + j] * 2 + i) * 2 * CH for j in range(rows)]
            held = [in_ref[pl.ds(at, 2 * CH), :].astype(jnp.float32) for at in spots]
            part = jnp.concatenate(held).T
            made[i, :, pl.ds(block * LANES, LANES)] = part.astype(jnp.bfloat16)
        copies.append(pltpu.make_async_copy(made.at[i], hbm, sems.at[i]))
        copies[-1].start()
    for copy in copies:
        copy.wait()


def mix(first, second):
    total = max(len(first), 1)
    done = 0
    for i, step in enumerate(first):
        step()
        while done < len(second) * (i + 1) // total:
            second[done]()
            done += 1
    for step in second[done:]:
        step()


def dft_steps(load, sign, store):
    parts = {}

    def inner(i):
        def step():
            parts[i] = dft([load(n) for n in range(i, BLOCKS, 4)], sign)
        return step

    def outer(k):
        def step():
            turned = [rotate(parts[i][k], sign * 2.0 * math.pi * i * k / BLOCKS) for i in range(4)]
            for j, value in enumerate(dft(turned, sign)):
                store(k + 8 * j, value)
        return step

    return [inner(i) for i in range(4)] + [outer(k) for k in range(8)]


def ahead(read, cos_ref, sin_ref, work, slab):
    def load(n):
        part, angle = read(n), math.pi * n / (2 * BLOCKS)
        return part * math.cos(angle), part * -math.sin(angle)

    def store(q, value):
        re, im = value
        cos, sin = cos_ref[q : q + 1, :], sin_ref[q : q + 1, :]
        rows = pl.ds((slab * BLOCKS + q) * CH, CH)
        work[rows, :LANES] = re * cos + im * sin
        work[rows, LANES:] = im * cos - re * sin

    return dft_steps(load, -1, store)


def lanes(work, spec, mat_ref, which, slab):
    def step(at):
        def run():
            rows = pl.ds(slab * BLOCKS * CH + at, PART)
            spec[rows] = product(work[rows], mat_ref[which])

        return run

    return [step(at) for at in range(0, BLOCKS * CH, PART)]


def field_kernel(in_ref, cos_ref, sin_ref, mat_ref, spec, work):
    def steps(a):
        made = []
        for slab in range(2):

            def read(n, slab=slab):
                held = in_ref[pl.ds((PLACE_IN[n] * 3 + a) * 2 * CH, 2 * CH), :].astype(jnp.float32)
                return held[slab * CH : (slab + 1) * CH]

            made += ahead(read, cos_ref, sin_ref, work.at[a], slab)
        return made

    inner = lambda a: [s for h in range(2) for s in lanes(work.at[a], spec.at[a], mat_ref, 0, h)]
    mix(steps(0), [])
    mix(steps(1), inner(0))
    mix(steps(2), inner(1))
    mix([], inner(2))


def operator_kernel(in_ref, spec, cos_ref, sin_ref, mat_ref, out_ref, work, other):
    size = BLOCKS * CH

    def steps(slab):
        def read(n):
            held = in_ref[pl.ds(PLACE_IN[n] * 2 * CH, 2 * CH), :].astype(jnp.float32)
            return held[slab * CH : (slab + 1) * CH]

        return ahead(read, cos_ref, sin_ref, work.at[2], slab)

    def multiply(slab):
        def step(at):
            def run():
                rows = pl.ds(slab * size + at, 64)
                re = spec[2, rows, :LANES] + other[2, rows, :LANES]
                im = spec[2, rows, LANES:] - other[2, rows, LANES:]
                for a, turn in enumerate((im, -im)):
                    has_re, has_im = spec[a, rows, :LANES], spec[a, rows, LANES:]
                    work[a, rows, :LANES] = re * has_re - turn * has_im
                    work[a, rows, LANES:] = re * has_im + turn * has_re

            return run

        return [step(at) for at in range(0, size, 64)]

    def back(a, slab):
        def load(q):
            cos, sin = cos_ref[q : q + 1, :], sin_ref[q : q + 1, :]
            rows = pl.ds(slab * size + q * CH, CH)
            re, im = other[a, rows, :LANES], other[a, rows, LANES:]
            return re * cos - im * sin, re * sin + im * cos

        def store(n, value):
            angle, scale = math.pi * n / (2 * BLOCKS), 2.0 / TOTAL
            re, im = value
            part = re * (math.cos(angle) * scale) - im * (math.sin(angle) * scale)
            kept = pl.ds(n * CH, CH)
            if slab == 0:
                work[2, kept, :LANES] = part
            else:
                both = jnp.concatenate([work[2, kept, :LANES], part])
                out_ref[pl.ds((PLACE_OUT[n] * 2 + a) * 2 * CH, 2 * CH), :] = both.astype(jnp.bfloat16)

        return dft_steps(load, 1, store)

    inner = lambda a, slab, which: lanes(work.at[a], other.at[a], mat_ref, which, slab)
    mix(steps(0), [])
    mix(steps(1), inner(2, 0, 0))
    mix(multiply(0), inner(2, 1, 0))
    mix(multiply(1), inner(0, 0, 1))
    mix(back(0, 0), inner(0, 1, 1))
    mix(back(0, 1), inner(1, 0, 1))
    mix(back(1, 0), inner(1, 1, 1))
    mix(back(1, 1), [])


def exchange(rows, order):
    return lax.all_to_all(
        rows, "ctx", split_axis=0, concat_axis=0, tiled=True, axis_index_groups=[list(order)]
    )


def body(tokens, cotangent, filters):
    cos, sin, matrices = tables()
    chans = tokens.shape[1]
    rows = 2 * BLOCKS * CH
    mirror = lax.axis_size("tp") // 2
    vmem = pl.BlockSpec(memory_space=pltpu.VMEM)
    hbm = pl.BlockSpec(memory_space=pltpu.HBM)
    fields = [pltpu.with_memory_space_constraint(x, pltpu.HBM) for x in (tokens, cotangent, filters)]
    sent = pl.pallas_call(
        gather_kernel,
        out_shape=pltpu.VMEM((3 * chans, LANES), jnp.bfloat16),
        in_specs=[hbm] * 3,
        out_specs=vmem,
        scratch_shapes=[pltpu.VMEM((3, LANES, chans), jnp.bfloat16), pltpu.SemaphoreType.DMA((3,))],
        compiler_params=PARAMS,
    )(*fields)
    held = exchange(sent, ORDER_IN)
    own = held.reshape(BLOCKS, 3, 2 * CH, LANES)[:, 2].reshape(rows, LANES)
    other = lax.ppermute(own, "tp", [(i, i ^ mirror) for i in range(2 * mirror)])
    spectra = pl.pallas_call(
        field_kernel,
        out_shape=pltpu.VMEM((3, rows, 2 * LANES), jnp.float32),
        in_specs=[vmem] * 4,
        out_specs=vmem,
        scratch_shapes=[pltpu.VMEM((3, rows, 2 * LANES), jnp.float32)],
        compiler_params=PARAMS,
        cost_estimate=pl.CostEstimate(flops=10**9, bytes_accessed=10**6, transcendentals=0),
    )(held, cos, sin, matrices)
    made = pl.pallas_call(
        operator_kernel,
        out_shape=pltpu.VMEM((2 * chans, LANES), jnp.bfloat16),
        in_specs=[vmem] * 5,
        out_specs=vmem,
        scratch_shapes=[pltpu.VMEM((3, rows, 2 * LANES), jnp.float32)] * 2,
        compiler_params=PARAMS,
        cost_estimate=pl.CostEstimate(flops=10**9, bytes_accessed=10**6, transcendentals=0),
    )(other, spectra, cos, sin, matrices)
    back = exchange(made, ORDER_OUT)
    return pl.pallas_call(
        scatter_kernel,
        out_shape=[jax.ShapeDtypeStruct((LANES, chans), jnp.bfloat16)] * 2,
        in_specs=[vmem],
        out_specs=[hbm] * 2,
        scratch_shapes=[pltpu.VMEM((2, LANES, chans), jnp.bfloat16), pltpu.SemaphoreType.DMA((2,))],
        compiler_params=PARAMS,
    )(back)


def solution(mesh):
    return jax.shard_map(
        body,
        mesh=mesh,
        in_specs=(P("ctx", "tp"),) * 3,
        out_specs=(P("ctx", "tp"),) * 2,
        check_vma=False,
    )
```

```python
import math

import jax
import jax.numpy as jnp
import numpy as np
from jax import lax
from jax.experimental import pallas as pl
from jax.experimental.pallas import tpu as pltpu
from jax.sharding import PartitionSpec as P

LANES = 128
BLOCKS = 32
TOTAL = 2 * LANES * BLOCKS
CH = 8
PART = 128
ORDER_IN = (29, 26, 10, 14, 23, 16, 17, 11, 24, 13, 20, 15, 22, 2, 7, 6, 30, 9, 19, 21, 28, 25, 18, 5, 0, 1, 27, 31, 12, 8, 3, 4)
ORDER_OUT = (4, 12, 24, 2, 28, 10, 18, 27, 21, 9, 19, 8, 6, 17, 13, 15, 29, 3, 5, 1, 7, 14, 0, 31, 20, 30, 26, 22, 25, 11, 23, 16)
PLACE_IN = tuple(ORDER_IN.index(n) for n in range(BLOCKS))
PLACE_OUT = tuple(ORDER_OUT.index(n) for n in range(BLOCKS))
PARAMS = pltpu.CompilerParams(vmem_limit_bytes=40 * 2**20)


def tables():
    q = np.arange(BLOCKS)[:, None]
    m = np.arange(LANES)[None, :]
    turn = 2.0 * math.pi * (2 * q + 0.5) * m / TOTAL
    lane = np.arange(LANES)
    phase = 2.0 * math.pi * (lane[:, None] * lane[None, :] % LANES) / LANES
    cos, sin = np.cos(phase), np.sin(phase)
    ahead = np.block([[cos, -sin], [sin, cos]]).astype(np.float32)
    halves = []
    for matrix in (ahead, ahead.T):
        high = matrix.astype(jnp.bfloat16)
        low = (matrix - high.astype(np.float32)).astype(jnp.bfloat16)
        halves.append(np.concatenate([high, high, low]))
    return np.cos(turn).astype(np.float32), np.sin(turn).astype(np.float32), np.stack(halves)


def rotate(value, angle):
    re, im = value
    eighth = round(angle / (math.pi / 4), 9) % 8
    root = math.sqrt(0.5)
    if eighth == 0:
        return re, im
    if eighth == 2:
        return -im, re
    if eighth == 4:
        return -re, -im
    if eighth == 6:
        return im, -re
    if eighth in (1, 3, 5, 7):
        plus, minus = (re + im) * root, (re - im) * root
        return {1: (minus, plus), 3: (-plus, minus), 5: (-minus, -plus), 7: (plus, -minus)}[eighth]
    cos, sin = math.cos(angle), math.sin(angle)
    return re * cos - im * sin, re * sin + im * cos


def dft(values, sign):
    size = len(values)
    if size == 1:
        return values
    if size == 2:
        (ar, ai), (br, bi) = values
        return [(ar + br, ai + bi), (ar - br, ai - bi)]
    radix = 4
    if size % 4 or size == 8:
        radix = 2
    rest = size // radix
    parts = [dft(values[i::radix], sign) for i in range(radix)]
    out = [None] * size
    for k in range(rest):
        turned = [rotate(parts[i][k], sign * 2.0 * math.pi * i * k / size) for i in range(radix)]
        if radix == 2:
            (ar, ai), (br, bi) = turned
            out[k], out[k + rest] = (ar + br, ai + bi), (ar - br, ai - bi)
        else:
            (ar, ai), (br, bi), (cr, ci), (dr, di) = turned
            er, ei, fr, fi = ar + cr, ai + ci, ar - cr, ai - ci
            gr, gi, hr, hi = br + dr, bi + di, (br - dr) * sign, (bi - di) * sign
            out[k] = er + gr, ei + gi
            out[k + rest] = fr - hi, fi + hr
            out[k + 2 * rest] = er - gr, ei - gi
            out[k + 3 * rest] = fr + hi, fi - hr
    return out


def product(left, matrix):
    high = left.astype(jnp.bfloat16)
    low = (left - high.astype(jnp.float32)).astype(jnp.bfloat16)
    parts = jnp.concatenate([high, low, high], axis=1)
    return jnp.dot(parts, matrix, preferred_element_type=jnp.float32)


def gather_kernel(tok_hbm, grad_hbm, filt_hbm, out_ref, held, sems):
    copies = []
    for i, hbm in enumerate((tok_hbm, grad_hbm, filt_hbm)):
        copies.append(pltpu.make_async_copy(hbm, held.at[i], sems.at[i]))
        copies[-1].start()
    for copy in copies:
        copy.wait()
    per = LANES // (2 * CH)
    for block in range(held.shape[2] // LANES):
        cols = pl.ds(block * LANES, LANES)
        turned = [held[i, :, cols].astype(jnp.float32).T for i in range(3)]
        for j in range(per):
            rows = [part[2 * CH * j : 2 * CH * (j + 1)] for part in turned]
            at = pl.ds(PLACE_IN[block * per + j] * 6 * CH, 6 * CH)
            out_ref[at, :] = jnp.concatenate(rows).astype(jnp.bfloat16)


def scatter_kernel(in_ref, out_hbm, grad_hbm, made, sems):
    rows = LANES // (2 * CH)
    copies = []
    for i, hbm in enumerate((out_hbm, grad_hbm)):
        for block in range(hbm.shape[1] // LANES):
            spots = [(PLACE_OUT[block * rows + j] * 2 + i) * 2 * CH for j in range(rows)]
            held = [in_ref[pl.ds(at, 2 * CH), :].astype(jnp.float32) for at in spots]
            part = jnp.concatenate(held).T
            made[i, :, pl.ds(block * LANES, LANES)] = part.astype(jnp.bfloat16)
        copies.append(pltpu.make_async_copy(made.at[i], hbm, sems.at[i]))
        copies[-1].start()
    for copy in copies:
        copy.wait()


def mix(first, second):
    total = max(len(first), 1)
    done = 0
    for i, step in enumerate(first):
        step()
        while done < len(second) * (i + 1) // total:
            second[done]()
            done += 1
    for step in second[done:]:
        step()


def dft_steps(load, sign, store):
    parts = {}

    def inner(i):
        def step():
            parts[i] = dft([load(n) for n in range(i, BLOCKS, 4)], sign)
        return step

    def outer(k):
        def step():
            turned = [rotate(parts[i][k], sign * 2.0 * math.pi * i * k / BLOCKS) for i in range(4)]
            for j, value in enumerate(dft(turned, sign)):
                store(k + 8 * j, value)
        return step

    return [inner(i) for i in range(4)] + [outer(k) for k in range(8)]


def ahead(read, cos_ref, sin_ref, work, slab):
    def load(n):
        part, angle = read(n), math.pi * n / (2 * BLOCKS)
        return part * math.cos(angle), part * -math.sin(angle)

    def store(q, value):
        re, im = value
        cos, sin = cos_ref[q : q + 1, :], sin_ref[q : q + 1, :]
        rows = pl.ds((slab * BLOCKS + q) * CH, CH)
        work[rows, :LANES] = re * cos + im * sin
        work[rows, LANES:] = im * cos - re * sin

    return dft_steps(load, -1, store)


def lanes(work, spec, mat_ref, which, slab):
    def step(at):
        def run():
            rows = pl.ds(slab * BLOCKS * CH + at, PART)
            spec[rows] = product(work[rows], mat_ref[which])

        return run

    return [step(at) for at in range(0, BLOCKS * CH, PART)]


def field_kernel(in_ref, cos_ref, sin_ref, mat_ref, spec, work):
    def steps(a):
        made = []
        for slab in range(2):

            def read(n, slab=slab):
                held = in_ref[pl.ds((PLACE_IN[n] * 3 + a) * 2 * CH, 2 * CH), :].astype(jnp.float32)
                return held[slab * CH : (slab + 1) * CH]

            made += ahead(read, cos_ref, sin_ref, work.at[a], slab)
        return made

    inner = lambda a: [s for h in range(2) for s in lanes(work.at[a], spec.at[a], mat_ref, 0, h)]
    mix(steps(0), [])
    mix(steps(1), inner(0))
    mix(steps(2), inner(1))
    mix([], inner(2))


def operator_kernel(in_ref, spec, cos_ref, sin_ref, mat_ref, out_ref, work, other):
    size = BLOCKS * CH

    def steps(slab):
        def read(n):
            held = in_ref[pl.ds(PLACE_IN[n] * 2 * CH, 2 * CH), :].astype(jnp.float32)
            return held[slab * CH : (slab + 1) * CH]

        return ahead(read, cos_ref, sin_ref, work.at[2], slab)

    def multiply(slab):
        def step(at):
            def run():
                rows = pl.ds(slab * size + at, 64)
                re = spec[2, rows, :LANES] + other[2, rows, :LANES]
                im = spec[2, rows, LANES:] - other[2, rows, LANES:]
                for a, turn in enumerate((im, -im)):
                    has_re, has_im = spec[a, rows, :LANES], spec[a, rows, LANES:]
                    work[a, rows, :LANES] = re * has_re - turn * has_im
                    work[a, rows, LANES:] = re * has_im + turn * has_re

            return run

        return [step(at) for at in range(0, size, 64)]

    def back(a, slab):
        def load(q):
            cos, sin = cos_ref[q : q + 1, :], sin_ref[q : q + 1, :]
            rows = pl.ds(slab * size + q * CH, CH)
            re, im = other[a, rows, :LANES], other[a, rows, LANES:]
            return re * cos - im * sin, re * sin + im * cos

        def store(n, value):
            angle, scale = math.pi * n / (2 * BLOCKS), 2.0 / TOTAL
            re, im = value
            part = re * (math.cos(angle) * scale) - im * (math.sin(angle) * scale)
            kept = pl.ds(n * CH, CH)
            if slab == 0:
                work[2, kept, :LANES] = part
            else:
                both = jnp.concatenate([work[2, kept, :LANES], part])
                out_ref[pl.ds((PLACE_OUT[n] * 2 + a) * 2 * CH, 2 * CH), :] = both.astype(jnp.bfloat16)

        return dft_steps(load, 1, store)

    inner = lambda a, slab, which: lanes(work.at[a], other.at[a], mat_ref, which, slab)
    mix(steps(0), [])
    mix(steps(1), inner(2, 0, 0))
    mix(multiply(0), inner(2, 1, 0))
    mix(multiply(1), inner(0, 0, 1) + inner(1, 0, 1))
    mix(back(0, 0), inner(0, 1, 1) + inner(1, 1, 1))
    mix(back(0, 1), [])
    mix(back(1, 0), [])
    mix(back(1, 1), [])


def exchange(rows, order):
    return lax.all_to_all(
        rows, "ctx", split_axis=0, concat_axis=0, tiled=True, axis_index_groups=[list(order)]
    )


def body(tokens, cotangent, filters):
    cos, sin, matrices = tables()
    chans = tokens.shape[1]
    rows = 2 * BLOCKS * CH
    mirror = lax.axis_size("tp") // 2
    vmem = pl.BlockSpec(memory_space=pltpu.VMEM)
    hbm = pl.BlockSpec(memory_space=pltpu.HBM)
    fields = [pltpu.with_memory_space_constraint(x, pltpu.HBM) for x in (tokens, cotangent, filters)]
    sent = pl.pallas_call(
        gather_kernel,
        out_shape=pltpu.VMEM((3 * chans, LANES), jnp.bfloat16),
        in_specs=[hbm] * 3,
        out_specs=vmem,
        scratch_shapes=[pltpu.VMEM((3, LANES, chans), jnp.bfloat16), pltpu.SemaphoreType.DMA((3,))],
        compiler_params=PARAMS,
    )(*fields)
    held = exchange(sent, ORDER_IN)
    own = held.reshape(BLOCKS, 3, 2 * CH, LANES)[:, 2].reshape(rows, LANES)
    other = lax.ppermute(own, "tp", [(i, i ^ mirror) for i in range(2 * mirror)])
    spectra = pl.pallas_call(
        field_kernel,
        out_shape=pltpu.VMEM((3, rows, 2 * LANES), jnp.float32),
        in_specs=[vmem] * 4,
        out_specs=vmem,
        scratch_shapes=[pltpu.VMEM((3, rows, 2 * LANES), jnp.float32)],
        compiler_params=PARAMS,
        cost_estimate=pl.CostEstimate(flops=10**9, bytes_accessed=10**6, transcendentals=0),
    )(held, cos, sin, matrices)
    made = pl.pallas_call(
        operator_kernel,
        out_shape=pltpu.VMEM((2 * chans, LANES), jnp.bfloat16),
        in_specs=[vmem] * 5,
        out_specs=vmem,
        scratch_shapes=[pltpu.VMEM((3, rows, 2 * LANES), jnp.float32)] * 2,
        compiler_params=PARAMS,
        cost_estimate=pl.CostEstimate(flops=10**9, bytes_accessed=10**6, transcendentals=0),
    )(other, spectra, cos, sin, matrices)
    back = exchange(made, ORDER_OUT)
    return pl.pallas_call(
        scatter_kernel,
        out_shape=[jax.ShapeDtypeStruct((LANES, chans), jnp.bfloat16)] * 2,
        in_specs=[vmem],
        out_specs=[hbm] * 2,
        scratch_shapes=[pltpu.VMEM((2, LANES, chans), jnp.bfloat16), pltpu.SemaphoreType.DMA((2,))],
        compiler_params=PARAMS,
    )(back)


def solution(mesh):
    return jax.shard_map(
        body,
        mesh=mesh,
        in_specs=(P("ctx", "tp"),) * 3,
        out_specs=(P("ctx", "tp"),) * 2,
        check_vma=False,
    )
```
